32 devices in a mesh: groups: 2 (over y), inst: 4 (over z), tp: 4 (over x, core).
Axes of the slice: x: 2, y: 2, z: 4, core: 2. Of those that a mesh axis runs over, the one named last changes fastest.
Arguments:
- key_value_pool: bfloat16 [272, 2, 8, 128, 128], P(('groups', 'inst'), None, 'tp'), parts along dimension 0, may hold values from -6 to 6
- key_value_scale: bfloat16 [272, 2, 8], P(('groups', 'inst'), None, 'tp'), parts along dimension 0, may hold values from 0.25 to 2
- lengths: int32 [64], P(('groups', 'inst')), parts along dimension 0, may hold values from 1 to 512, as said below
- table: int32 [64, 4], P(('groups', 'inst')), parts along dimension 0, may hold values from 0 to 33, as said below
- moves: int32 [16, 3], P('groups'), parts along dimension 0, may hold values from 0 to 33, as said below
- queries: bfloat16 [64, 4, 8192], P(('groups', 'inst'), None, 'tp'), parts along dimension 0, may hold values from -200 to 200
- new_kv: bfloat16 [64, 4, 2, 1024], P(('groups', 'inst'), None, None, 'tp'), parts along dimension 0, may hold values from -7 to 7
Outputs:
- attended: bfloat16 [64, 4, 8192], P(('groups', 'inst'), None, 'tp'), parts along dimension 0
- landed: bfloat16 [16, 2, 8, 128, 128], P(('groups', 'inst'), None, 'tp'), parts along dimension 0
- arrival_scales: bfloat16 [16, 2, 8], P(('groups', 'inst'), None, 'tp'), parts along dimension 0
- load: float32 [8], P(('groups', 'inst')), parts along dimension 0
The draws below stay inside these ranges and needn't reach their ends.
There are 2 independent parts, one for each index of `groups`. The reference program is written for one: setup_inputs(seed, part) draws one part's arguments, and reference() takes and returns one part's arrays. A program takes and returns all parts, laid end to end along the dimension named above; each array names one. Nothing has to cross between parts.
Inputs may be any that keep to these rules, and one draw needn't show every extreme that they name: `lengths`: in every draw some slot that receives a migrated request holds 512 tokens. `table`: row b lists pool blocks of its own instance; block j holds tokens j * 128 to (j+1) * 128 - 1; the entries of one instance's rows are distinct; entries past a request's last block are not read. `moves`: row r: the source pool block holding the last block of the request leaving instance s = r // 2, its destination instance (s + 1 + r % 2) mod 4, and its destination slot; every instance receives 2 rows, with distinct slots; a source block is used by no table row of its instance.
All inputs are finite; a program needn't handle non-finite values.
Results may differ from the reference program's by a relative error of at most 0.0049.
Values may be sent and summed in bfloat16 or wider, within the bound.
A program may use at most 64 MiB of HBM per device.

```python
import math
import jax
import jax.numpy as jnp
from jax import lax

QUERY_HEADS = 64
KEY_VALUE_HEADS = 8
HEAD_SIZE = 128
BLOCK_TOKENS = 128
DECODE_STEPS = 4
REQUEST_BLOCKS = 4
LEAVING_COUNT = 2
BATCH_SLOTS = 8
GROUP_QUERIES = 8
POOL_BLOCKS = 34
N_INST = 4


def layout(key):
    random_subkeys = jax.random.split(key, 6)

    def shuffle_slots(subkey):
        return jax.random.permutation(subkey, BATCH_SLOTS).astype(jnp.int32)

    def shuffle_pool(subkey):
        return jax.random.permutation(subkey, POOL_BLOCKS).astype(jnp.int32)
    slot_order = jax.vmap(shuffle_slots)(jax.random.split(random_subkeys[1], N_INST))
    pool_order = jax.vmap(shuffle_pool)(jax.random.split(random_subkeys[2], N_INST))
    picked_source = jax.random.randint(random_subkeys[5], (), 0, N_INST, dtype=jnp.int32)
    source_row = pool_order[picked_source]
    leave_position = BATCH_SLOTS * REQUEST_BLOCKS
    top_position = jnp.argmax(source_row == POOL_BLOCKS - 1).astype(jnp.int32)
    displaced = source_row[leave_position]
    source_row = source_row.at[top_position].set(displaced).at[leave_position].set(POOL_BLOCKS - 1)
    pool_order = pool_order.at[picked_source].set(source_row)
    all_rows = jnp.arange(N_INST * LEAVING_COUNT, dtype=jnp.int32)
    sources = all_rows // LEAVING_COUNT
    mover = all_rows % LEAVING_COUNT
    targets = (sources + mover + 1) % N_INST
    target_slot = slot_order[targets, mover]
    source_block = pool_order[sources, BATCH_SLOTS * REQUEST_BLOCKS + mover]
    ceiling = BLOCK_TOKENS + (REQUEST_BLOCKS * BLOCK_TOKENS - BLOCK_TOKENS) * (jnp.arange(N_INST, dtype=jnp.int32) + 1) // N_INST
    drawn_sample = jax.random.randint(random_subkeys[3], (N_INST, BATCH_SLOTS), 0, 1 << 20, dtype=jnp.int32)
    length = drawn_sample % ceiling[:, None] + 1
    chosen = jax.random.randint(random_subkeys[4], (), 0, N_INST, dtype=jnp.int32)
    length = length.at[chosen, slot_order[chosen, 0]].set(REQUEST_BLOCKS * BLOCK_TOKENS)
    tab = pool_order[:, :BATCH_SLOTS * REQUEST_BLOCKS].reshape(N_INST * BATCH_SLOTS, REQUEST_BLOCKS)
    listing = jnp.stack([source_block, targets, target_slot], axis=1)
    return (length.reshape(N_INST * BATCH_SLOTS), tab, listing)


def fresh_tokens(key):
    drawn_sample = jax.random.normal(key, (N_INST * BATCH_SLOTS, DECODE_STEPS, 2, KEY_VALUE_HEADS * HEAD_SIZE), jnp.float32)
    return jnp.clip(drawn_sample, -6.0, 6.0)


def draw_lengths(key, part):
    shared = layout(key)
    return shared[0]


def draw_table(key, part):
    shared = layout(key)
    return shared[1]


def draw_moves(key, part):
    shared = layout(key)
    return shared[2]


def draw_new_kv(key, part):
    base_offset = fresh_tokens(key)
    return base_offset.astype(jnp.bfloat16)


def draw_queries(key, part):
    key = jax.random.fold_in(key, 9)
    random_subkeys = jax.random.split(key, 1)
    request_list = N_INST * BATCH_SLOTS
    value_rows = jnp.clip(jax.random.normal(random_subkeys[0], (request_list, DECODE_STEPS, QUERY_HEADS * HEAD_SIZE), jnp.float32), -6.0, 6.0)
    return value_rows.astype(jnp.bfloat16)


def steps_of(key, dims, cuts, smallest, high):
    def one(axis_at, parts):
        draws = jax.random.uniform(jax.random.fold_in(jax.random.fold_in(key, 6), axis_at), (parts,), jnp.float32, smallest / len(cuts), high / len(cuts))
        return jnp.repeat(jnp.exp(draws), dims[axis_at] // parts).reshape((-1,) + (1,) * (len(dims) - axis_at - 1))

    level = one(*cuts[0])
    for cut in cuts[1:]:
        level = level * one(*cut)
    return level


def normal_values(rng, dims, scale, limit, shards=(), held_as=jnp.bfloat16):
    result = scale * jax.random.normal(rng, dims, jnp.float32)
    if shards:
        result = result * steps_of(rng, dims, shards, -0.22, 0.18)
    return jnp.clip(result, -limit, limit).astype(held_as)


def setup_inputs(seed: int = 0, part: int = 0) -> dict:
    key_list = jax.random.split(jax.random.key(seed), 8)
    part_keys = jax.random.split(jax.random.fold_in(key_list[7], part), 8)
    key_value_pool = normal_values(part_keys[0], (N_INST * POOL_BLOCKS, 2, KEY_VALUE_HEADS, BLOCK_TOKENS, HEAD_SIZE), 1.0, 6.0, ((0, 4), (2, 4)))
    key_value_scale = jnp.clip(jnp.exp(math.log(2.0) - 2.0794415 * jax.random.uniform(part_keys[1], (N_INST * POOL_BLOCKS, 2, KEY_VALUE_HEADS), jnp.float32) ** steps_of(part_keys[1], (N_INST * POOL_BLOCKS, 2, KEY_VALUE_HEADS), ((0, 4), (2, 4)), -0.2, 0.2)), 0.25, 2.0).astype(jnp.bfloat16)
    lengths = draw_lengths(jax.random.fold_in(jax.random.fold_in(key_list[7], part), 71), part)
    table = draw_table(jax.random.fold_in(jax.random.fold_in(key_list[7], part), 71), part)
    moves = draw_moves(jax.random.fold_in(jax.random.fold_in(key_list[7], part), 71), part)
    queries = draw_queries(jax.random.fold_in(jax.random.fold_in(key_list[7], part), 71), part)
    new_kv = draw_new_kv(jax.random.fold_in(jax.random.fold_in(key_list[7], part), 71), part)
    return dict(key_value_pool=key_value_pool, key_value_scale=key_value_scale, lengths=lengths, table=table, moves=moves, queries=queries, new_kv=new_kv)


def reference(key_value_pool, key_value_scale, lengths, table, moves, queries, new_kv):
    all_rows = jnp.arange(N_INST * LEAVING_COUNT, dtype=jnp.int32)
    sources = all_rows // LEAVING_COUNT
    targets = moves[:, 1]
    before = (targets[:, None] == targets[None, :]) & (all_rows[:, None] > all_rows[None, :])
    rank = lax.optimization_barrier(jnp.sum(before.astype(jnp.int32), axis=1))
    place_index = targets * LEAVING_COUNT + rank
    sender_rows = sources * POOL_BLOCKS + moves[:, 0]
    landed = jnp.zeros((N_INST * LEAVING_COUNT, 2, KEY_VALUE_HEADS, BLOCK_TOKENS, HEAD_SIZE), key_value_pool.dtype).at[place_index].set(key_value_pool[sender_rows])
    arrival_scales = jnp.zeros((N_INST * LEAVING_COUNT, 2, KEY_VALUE_HEADS), key_value_scale.dtype).at[place_index].set(key_value_scale[sender_rows])
    incoming = jnp.full((N_INST * BATCH_SLOTS,), -1, jnp.int32).at[targets * BATCH_SLOTS + moves[:, 2]].set(rank)
    scaling = 1.0 / math.sqrt(HEAD_SIZE)

    def instance(block_index):
        tab = lax.dynamic_slice_in_dim(table, block_index * BATCH_SLOTS, BATCH_SLOTS, 0)
        length = lax.dynamic_slice_in_dim(lengths, block_index * BATCH_SLOTS, BATCH_SLOTS, 0)
        arrival = lax.dynamic_slice_in_dim(incoming, block_index * BATCH_SLOTS, BATCH_SLOTS, 0)
        blocks = key_value_pool[block_index * POOL_BLOCKS + tab].astype(jnp.float32)
        scales = key_value_scale[block_index * POOL_BLOCKS + tab].astype(jnp.float32)
        counts = (length + BLOCK_TOKENS - 1) // BLOCK_TOKENS
        last_block = (jnp.arange(REQUEST_BLOCKS, dtype=jnp.int32)[None, :] == counts[:, None] - 1) & (arrival >= 0)[:, None]
        local_landed = lax.dynamic_slice_in_dim(landed, block_index * LEAVING_COUNT, LEAVING_COUNT, 0)
        local_scale = lax.dynamic_slice_in_dim(arrival_scales, block_index * LEAVING_COUNT, LEAVING_COUNT, 0)
        here = local_landed[jnp.maximum(arrival, 0)].astype(jnp.float32)
        here_scale = local_scale[jnp.maximum(arrival, 0)].astype(jnp.float32)
        blocks = jnp.where(last_block[:, :, None, None, None, None], here[:, None], blocks)
        scales = jnp.where(last_block[:, :, None, None], here_scale[:, None], scales)
        cache_keys = blocks[:, :, 0] * scales[:, :, 0][:, :, :, None, None]
        cache_values = blocks[:, :, 1] * scales[:, :, 1][:, :, :, None, None]
        query_head_rows = lax.dynamic_slice_in_dim(queries, block_index * BATCH_SLOTS, BATCH_SLOTS, 0).astype(jnp.float32).reshape(BATCH_SLOTS, DECODE_STEPS, KEY_VALUE_HEADS, GROUP_QUERIES, HEAD_SIZE)
        fresh_entries = lax.dynamic_slice_in_dim(new_kv, block_index * BATCH_SLOTS, BATCH_SLOTS, 0).astype(jnp.float32)
        newest_keys = fresh_entries[:, :, 0].reshape(BATCH_SLOTS, DECODE_STEPS, KEY_VALUE_HEADS, HEAD_SIZE)
        newest_values = fresh_entries[:, :, 1].reshape(BATCH_SLOTS, DECODE_STEPS, KEY_VALUE_HEADS, HEAD_SIZE)
        cached_score_rows = jnp.einsum('sthgd,sjhkd->sthgjk', query_head_rows, cache_keys) * scaling
        cached_score_rows = cached_score_rows.reshape(BATCH_SLOTS, DECODE_STEPS, KEY_VALUE_HEADS, GROUP_QUERIES, REQUEST_BLOCKS * BLOCK_TOKENS)
        fresh_scores = jnp.einsum('sthgd,suhd->sthgu', query_head_rows, newest_keys) * scaling
        positions = jnp.arange(REQUEST_BLOCKS * BLOCK_TOKENS, dtype=jnp.int32)
        cache_ok = jnp.broadcast_to((positions[None, :] < length[:, None])[:, None, None, None, :], cached_score_rows.shape)
        steps_ids = jnp.arange(DECODE_STEPS, dtype=jnp.int32)
        fresh_ok = jnp.broadcast_to((steps_ids[None, :] <= steps_ids[:, None])[None, :, None, None, :], fresh_scores.shape)
        scores = jnp.concatenate([cached_score_rows, fresh_scores], axis=-1)
        allowed = jnp.concatenate([cache_ok, fresh_ok], axis=-1)
        masked = jnp.where(allowed, scores, -1e+30)
        highest = lax.optimization_barrier(jnp.max(masked, axis=-1, keepdims=True))
        expsum = jnp.exp(masked - highest)
        weight_rows = expsum / lax.optimization_barrier(jnp.sum(expsum, axis=-1, keepdims=True))
        weight_rows = lax.optimization_barrier(weight_rows.astype(jnp.bfloat16)).astype(jnp.float32)
        cached_weight_rows = weight_rows[..., :REQUEST_BLOCKS * BLOCK_TOKENS].reshape(BATCH_SLOTS, DECODE_STEPS, KEY_VALUE_HEADS, GROUP_QUERIES, REQUEST_BLOCKS, BLOCK_TOKENS)
        fresh_weights = weight_rows[..., REQUEST_BLOCKS * BLOCK_TOKENS:]
        mixed = jnp.einsum('sthgjk,sjhkd->sthgd', cached_weight_rows, cache_values)
        mixed = mixed + jnp.einsum('sthgu,suhd->sthgd', fresh_weights, newest_values)
        return mixed.reshape(BATCH_SLOTS, DECODE_STEPS, QUERY_HEADS * HEAD_SIZE).astype(jnp.bfloat16)
    attended = lax.map(instance, jnp.arange(N_INST, dtype=jnp.int32)).reshape(N_INST * BATCH_SLOTS, DECODE_STEPS, QUERY_HEADS * HEAD_SIZE)
    tokens = lax.optimization_barrier(jnp.sum((lengths + DECODE_STEPS).reshape(N_INST, BATCH_SLOTS).astype(jnp.float32), axis=1))
    load = tokens / jnp.mean(tokens)
    return (attended, landed, arrival_scales, load)
```

```python
import functools
import math

import jax
import jax.numpy as jnp
from jax import lax
from jax.experimental import pallas as pl
from jax.experimental.pallas import tpu as pltpu
from jax.sharding import PartitionSpec as P

NEG = -1e30
TRANS = (((1,), (1,)), ((), ()))


def kernel(
    n, pool_hbm, scale_hbm, lengths, table, moves, q_hbm, new_hbm,
    out_ref, landed_hbm, aux_ref,
    pool, scale, q_ref, new_ref, staged, arrived, note, notes, qs, acc_s, m_s, l_s,
    pool_sem, in_sem, send_sem, recv_sem, note_send, note_recv, land_sem,
):
    me = lax.axis_index("inst")
    slots, steps, _ = q_ref.shape
    per = staged.shape[0]
    blocks = table.shape[1]
    heads, block_len, dim = pool.shape[2:]
    group = q_ref.shape[2] // (heads * dim)
    rows = group * steps
    width = group * dim
    scaling = 1.0 / math.sqrt(dim)

    pool_copy = pltpu.make_async_copy(pool_hbm, pool, pool_sem)
    pool_copy.start()
    scale_copy = pltpu.make_async_copy(scale_hbm, scale, in_sem.at[0])
    scale_copy.start()
    q_copy = pltpu.make_async_copy(q_hbm, q_ref, in_sem.at[1])
    q_copy.start()
    new_copy = pltpu.make_async_copy(new_hbm, new_ref, in_sem.at[2])
    new_copy.start()

    barrier = pltpu.get_barrier_semaphore()
    for k in range(1, n):
        pl.semaphore_signal(
            barrier, inc=1, device_id={"inst": lax.rem(me + k, n)},
            device_id_type=pl.DeviceIdType.MESH,
        )

    tokens = jnp.float32(0.0)
    for s in range(slots):
        tokens = tokens + (lengths[s] + steps).astype(jnp.float32)
    note[per] = jnp.full((8, 128), tokens, jnp.float32)
    scale_copy.wait()
    for j in range(per):
        pair = scale[moves[me * per + j, 0]].astype(jnp.float32)
        for kv in range(2):
            for h in range(heads):
                note[j, pl.ds(kv * heads + h, 1), :] = jnp.broadcast_to(
                    pair[kv : kv + 1, h : h + 1], (1, 128)
                )
    pool_copy.wait()
    for j in range(per):
        staged[j] = pool[moves[me * per + j, 0]]
    pl.semaphore_wait(barrier, n - 1)

    sends = []
    for j in range(per):
        for kv in range(2):
            sends.append(
                pltpu.make_async_remote_copy(
                    src_ref=staged.at[j, kv], dst_ref=arrived.at[j, kv],
                    send_sem=send_sem.at[j, kv], recv_sem=recv_sem.at[j, kv],
                    device_id={"inst": lax.rem(me + 1 + j, n)},
                    device_id_type=pl.DeviceIdType.MESH,
                )
            )
    note_sends = []
    for k in range(1, n):
        note_sends.append(
            pltpu.make_async_remote_copy(
                src_ref=note, dst_ref=notes.at[k - 1],
                send_sem=note_send.at[k - 1], recv_sem=note_recv.at[k - 1],
                device_id={"inst": lax.rem(me + k, n)},
                device_id_type=pl.DeviceIdType.MESH,
            )
        )
    for copy in note_sends + sends:
        copy.start()

    sources = [lax.rem(me + n - 1 - j, n) for j in range(per)]
    arrival_rows = [sources[j] * per + j for j in range(per)]
    total_rows = n * per
    ranks = []
    for j in range(per):
        rank = 0
        for i in range(per):
            if i != j:
                rank = rank + (arrival_rows[j] - arrival_rows[i] + total_rows) // total_rows
        ranks.append(rank)
    arrival_slots = [moves[arrival_rows[j], 2] for j in range(per)]

    lane = lax.broadcasted_iota(jnp.int32, (rows, block_len), 1)
    step_of = lax.broadcasted_iota(jnp.int32, (rows, block_len), 0) % steps
    causal = lane <= step_of
    q_copy.wait()
    new_copy.wait()

    def to_lanes(o):
        return jnp.concatenate(
            [o[g * steps : (g + 1) * steps] for g in range(group)], axis=1
        ).astype(jnp.bfloat16)

    def one_slot(s, carry):
        length = lengths[s]
        count = lax.div(length + (block_len - 1), block_len)
        hit = arrival_slots[0] == s
        for j in range(1, per):
            hit = jnp.logical_or(hit, arrival_slots[j] == s)
        limit = jnp.where(hit, (count - 1) * block_len, length)
        q_all = q_ref[s].astype(jnp.float32)
        fresh = [new_ref[s, u].astype(jnp.float32) for u in range(steps)]
        index = [jnp.clip(table[s, j], 0, pool.shape[0] - 1) for j in range(blocks)]
        scales = [scale[index[j]].astype(jnp.float32) for j in range(blocks)]
        pad = jnp.zeros((block_len - steps, dim), jnp.float32)
        for h in range(heads):
            lo = h * group * dim
            qh = jnp.concatenate(
                [q_all[:, lo + g * dim : lo + (g + 1) * dim] for g in range(group)], axis=0
            ).astype(jnp.bfloat16)
            qs[s, h] = qh
            new_k, new_v = [
                jnp.concatenate(
                    [f[kv : kv + 1, h * dim : (h + 1) * dim] for f in fresh] + [pad], axis=0
                ).astype(jnp.bfloat16)
                for kv in range(2)
            ]
            scored = []
            for j in range(blocks):
                raw = lax.dot_general(
                    qh, pool[index[j], 0, h], TRANS, preferred_element_type=jnp.float32
                )
                raw = raw * (scales[j][0:1, h : h + 1] * scaling)
                scored.append(jnp.where(lane + j * block_len < limit, raw, NEG))
            raw = lax.dot_general(qh, new_k, TRANS, preferred_element_type=jnp.float32)
            scored.append(jnp.where(causal, raw * scaling, NEG))
            top = scored[0]
            for x in scored[1:]:
                top = jnp.maximum(top, x)
            top = jnp.max(top, axis=1, keepdims=True)
            p = [jnp.exp(x - top) for x in scored]
            norm = p[0]
            for x in p[1:]:
                norm = norm + x
            norm = jnp.sum(norm, axis=1, keepdims=True)
            acc = jnp.dot(p[-1].astype(jnp.bfloat16), new_v, preferred_element_type=jnp.float32)
            for j in range(blocks):
                w = (p[j] * scales[j][1:2, h : h + 1]).astype(jnp.bfloat16)
                acc = acc + jnp.dot(
                    w, pool[index[j], 1, h], preferred_element_type=jnp.float32
                )
            acc_s[s, h] = acc
            m_s[s, h] = jnp.broadcast_to(top, (rows, dim))
            l_s[s, h] = jnp.broadcast_to(norm, (rows, dim))
            out_ref[s, :, h * width : (h + 1) * width] = to_lanes(acc / norm)
        return carry

    lax.fori_loop(0, slots, one_slot, 0)

    for copy in note_sends:
        copy.wait()
    total = note[per]
    for k in range(n - 1):
        total = total + notes[k, per]
    aux_ref[per] = note[per] * n / total

    flushes = []
    for j in range(per):
        aux_ref[ranks[j]] = notes[j, j]
        slot = arrival_slots[j]
        length = lengths[slot]
        start = lax.div(length - 1, block_len) * block_len
        for kv in range(2):
            sends[2 * j + kv].wait_recv()
            flush = pltpu.make_async_copy(
                arrived.at[j, kv], landed_hbm.at[ranks[j], kv], land_sem.at[j, kv]
            )
            flush.start()
            flushes.append(flush)
        for h in range(heads):
            key_scale = notes[j, j, pl.ds(h, 1), :] * scaling
            value_scale = notes[j, j, pl.ds(heads + h, 1), :]
            raw = lax.dot_general(
                qs[slot, h], arrived[j, 0, h], TRANS, preferred_element_type=jnp.float32
            )
            x = jnp.where(lane + start < length, raw * key_scale, NEG)
            old = m_s[slot, h]
            top = jnp.maximum(old, jnp.max(x, axis=1, keepdims=True))
            fade = jnp.exp(old - top)
            p = jnp.exp(x - top)
            norm = l_s[slot, h] * fade + jnp.sum(p, axis=1, keepdims=True)
            acc = acc_s[slot, h] * fade + jnp.dot(
                (p * value_scale).astype(jnp.bfloat16), arrived[j, 1, h],
                preferred_element_type=jnp.float32,
            )
            o = to_lanes(acc / norm)
            for s in range(slots):
                part = (s, slice(None), slice(h * width, (h + 1) * width))
                out_ref[part] = jnp.where(slot == s, o, out_ref[part])
    for copy in sends:
        copy.wait_send()
    for flush in flushes:
        flush.wait()


def local(pool, scale, lengths, table, moves, queries, new_kv):
    n = lax.axis_size("inst")
    per = moves.shape[0] // n
    slots, steps, _ = queries.shape
    heads, block_len, dim = pool.shape[2:]
    rows = queries.shape[2] // (heads * dim) * steps
    any_space = pl.BlockSpec(memory_space=pl.ANY)
    smem = pl.BlockSpec(memory_space=pltpu.SMEM)
    vmem = pl.BlockSpec(memory_space=pltpu.VMEM)
    bf16, f32 = jnp.bfloat16, jnp.float32
    attended, landed, aux = pl.pallas_call(
        functools.partial(kernel, n),
        out_shape=(
            jax.ShapeDtypeStruct(queries.shape, bf16),
            jax.ShapeDtypeStruct((per,) + pool.shape[1:], bf16),
            jax.ShapeDtypeStruct((per + 1, 8, 128), f32),
        ),
        in_specs=[any_space, any_space, smem, smem, smem, any_space, any_space],
        out_specs=(vmem, any_space, vmem),
        scratch_shapes=[
            pltpu.VMEM(pool.shape, bf16),
            pltpu.VMEM(scale.shape, bf16),
            pltpu.VMEM(queries.shape, bf16),
            pltpu.VMEM(new_kv.shape, bf16),
            pltpu.VMEM((per,) + pool.shape[1:], bf16),
            pltpu.VMEM((per,) + pool.shape[1:], bf16),
            pltpu.VMEM((per + 1, 8, 128), f32),
            pltpu.VMEM((n - 1, per + 1, 8, 128), f32),
            pltpu.VMEM((slots, heads, rows, dim), bf16),
            pltpu.VMEM((slots, heads, rows, dim), f32),
            pltpu.VMEM((slots, heads, rows, dim), f32),
            pltpu.VMEM((slots, heads, rows, dim), f32),
            pltpu.SemaphoreType.DMA,
            pltpu.SemaphoreType.DMA((3,)),
            pltpu.SemaphoreType.DMA((per, 2)),
            pltpu.SemaphoreType.DMA((per, 2)),
            pltpu.SemaphoreType.DMA((n - 1,)),
            pltpu.SemaphoreType.DMA((n - 1,)),
            pltpu.SemaphoreType.DMA((per, 2)),
        ],
        compiler_params=pltpu.CompilerParams(
            collective_id=0, has_side_effects=True, vmem_limit_bytes=32 * 1024 * 1024
        ),
    )(pool, scale, lengths, table, moves, queries, new_kv)
    arrival_scales = aux[:per, : 2 * heads, 0].reshape(per, 2, heads).astype(bf16)
    load = aux[per, 0, :1]
    return attended, landed, arrival_scales, load


def solution(mesh):
    both = ("groups", "inst")
    return jax.shard_map(
        local,
        mesh=mesh,
        in_specs=(
            P(both, None, "tp", None, None),
            P(both, None, "tp"),
            P(both),
            P(both, None),
            P("groups", None),
            P(both, None, "tp"),
            P(both, None, None, "tp"),
        ),
        out_specs=(
            P(both, None, "tp"),
            P(both, None, "tp", None, None),
            P(both, None, "tp"),
            P(both),
        ),
        check_vma=False,
    )
```

```python
import functools
import math

import jax
import jax.numpy as jnp
from jax import lax
from jax.experimental import pallas as pl
from jax.experimental.pallas import tpu as pltpu
from jax.sharding import PartitionSpec as P

NEG = -1e30
TRANS = (((1,), (1,)), ((), ()))


def to_lanes(o, steps):
    return jnp.concatenate(
        [o[i : i + steps] for i in range(0, o.shape[0], steps)], axis=1
    ).astype(jnp.bfloat16)


def kernel(
    n, pool_hbm, scale_hbm, lengths_hbm, table_hbm, moves_hbm, q_hbm, new_hbm,
    out_ref, arrived, q_out, acc_out, m_out, l_out, info_ref, load_ref,
    pool, scale, lengths, table, moves, q_ref, new_ref, staged, note, notes, qs, acc_s, m_s, l_s,
    pool_sem, in_sem, send_sem, recv_sem, note_send, note_recv,
):
    me = lax.axis_index("inst")
    slots, steps, _ = q_ref.shape
    per = staged.shape[0]
    blocks = table.shape[0]
    heads, block_len, dim = pool.shape[2:]
    group = q_ref.shape[2] // (heads * dim)
    rows = group * steps
    width = group * dim
    scaling = 1.0 / math.sqrt(dim)

    barrier = pltpu.get_barrier_semaphore()
    for k in range(1, n):
        pl.semaphore_signal(
            barrier, inc=1, device_id={"inst": lax.rem(me + k, n)},
            device_id_type=pl.DeviceIdType.MESH,
        )
    small = [
        pltpu.make_async_copy(x, y, in_sem.at[3 + i])
        for i, (x, y) in enumerate(
            ((moves_hbm, moves), (lengths_hbm, lengths), (table_hbm, table))
        )
    ]
    for copy in small:
        copy.start()
    pool_copy = pltpu.make_async_copy(pool_hbm, pool, pool_sem)
    pool_copy.start()
    scale_copy = pltpu.make_async_copy(scale_hbm, scale, in_sem.at[0])
    scale_copy.start()
    q_copy = pltpu.make_async_copy(q_hbm, q_ref, in_sem.at[1])
    q_copy.start()
    new_copy = pltpu.make_async_copy(new_hbm, new_ref, in_sem.at[2])
    new_copy.start()

    for copy in small:
        copy.wait()

    tokens = jnp.float32(0.0)
    for s in range(slots):
        tokens = tokens + (lengths[s] + steps).astype(jnp.float32)
    note[per] = jnp.full((8, 128), tokens, jnp.float32)
    scale_copy.wait()
    scale_rows = jnp.concatenate(
        [scale[kv].astype(jnp.float32) for kv in range(2)], axis=0
    )
    block_of = lax.broadcasted_iota(jnp.int32, scale_rows.shape, 1)

    def block_scale(index):
        return jnp.sum(
            jnp.where(block_of == index, scale_rows, 0.0), axis=1, keepdims=True
        )

    head_lane = lax.broadcasted_iota(jnp.int32, (1, 128), 1)
    for j in range(per):
        pair = block_scale(moves[0, me * per + j])
        for kv in range(2):
            row = jnp.zeros((1, 128), jnp.float32)
            for h in range(heads):
                r = kv * heads + h
                row = jnp.where(head_lane == h, pair[r : r + 1], row)
            note[j, pl.ds(kv, 1), :] = row
    pool_copy.wait()
    for j in range(per):
        staged[j] = pool[moves[0, me * per + j]]
    pl.semaphore_wait(barrier, n - 1)

    sends = []
    for j in range(per):
        for kv in range(2):
            sends.append(
                pltpu.make_async_remote_copy(
                    src_ref=staged.at[j, kv], dst_ref=arrived.at[j, kv],
                    send_sem=send_sem.at[j, kv], recv_sem=recv_sem.at[j, kv],
                    device_id={"inst": lax.rem(me + 1 + j, n)},
                    device_id_type=pl.DeviceIdType.MESH,
                )
            )
    note_sends = []
    for k in range(1, n):
        note_sends.append(
            pltpu.make_async_remote_copy(
                src_ref=note, dst_ref=notes.at[k - 1],
                send_sem=note_send.at[k - 1], recv_sem=note_recv.at[k - 1],
                device_id={"inst": lax.rem(me + k, n)},
                device_id_type=pl.DeviceIdType.MESH,
            )
        )
    for copy in note_sends + sends:
        copy.start()

    sources = [lax.rem(me + n - 1 - j, n) for j in range(per)]
    arrival_rows = [sources[j] * per + j for j in range(per)]
    arrival_slots = [moves[2, arrival_rows[j]] for j in range(per)]

    lane = lax.broadcasted_iota(jnp.int32, (rows, block_len), 1)
    step_of = lax.broadcasted_iota(jnp.int32, (rows, block_len), 0) % steps
    causal = lane <= step_of
    q_copy.wait()
    new_copy.wait()

    def one_slot(s, carry):
        length = lengths[s]
        count = lax.div(length + (block_len - 1), block_len)
        hit = arrival_slots[0] == s
        for j in range(1, per):
            hit = jnp.logical_or(hit, arrival_slots[j] == s)
        limit = jnp.where(hit, (count - 1) * block_len, length)
        q_all = q_ref[s].astype(jnp.float32)
        fresh = [new_ref[s, u].astype(jnp.float32) for u in range(steps)]
        index = [jnp.clip(table[j, s], 0, pool.shape[0] - 1) for j in range(blocks)]
        scales = [block_scale(index[j]) for j in range(blocks)]
        pad = jnp.zeros((block_len - steps, dim), jnp.float32)
        for h in range(heads):
            lo = h * group * dim
            qh = jnp.concatenate(
                [q_all[:, lo + g * dim : lo + (g + 1) * dim] for g in range(group)], axis=0
            ).astype(jnp.bfloat16)
            qs[s, h] = qh
            new_k, new_v = [
                jnp.concatenate(
                    [f[kv : kv + 1, h * dim : (h + 1) * dim] for f in fresh] + [pad], axis=0
                ).astype(jnp.bfloat16)
                for kv in range(2)
            ]
            scored = []
            for j in range(blocks):
                raw = lax.dot_general(
                    qh, pool[index[j], 0, h], TRANS, preferred_element_type=jnp.float32
                )
                raw = raw * (scales[j][h : h + 1] * scaling)
                scored.append(jnp.where(lane + j * block_len < limit, raw, NEG))
            raw = lax.dot_general(qh, new_k, TRANS, preferred_element_type=jnp.float32)
            scored.append(jnp.where(causal, raw * scaling, NEG))
            top = scored[0]
            for x in scored[1:]:
                top = jnp.maximum(top, x)
            top = jnp.max(top, axis=1, keepdims=True)
            p = [jnp.exp(x - top) for x in scored]
            norm = p[0]
            for x in p[1:]:
                norm = norm + x
            norm = jnp.sum(norm, axis=1, keepdims=True)
            acc = jnp.dot(p[-1].astype(jnp.bfloat16), new_v, preferred_element_type=jnp.float32)
            for j in range(blocks):
                w = (p[j] * scales[j][heads + h : heads + h + 1]).astype(jnp.bfloat16)
                acc = acc + jnp.dot(
                    w, pool[index[j], 1, h], preferred_element_type=jnp.float32
                )
            acc_s[s, h] = acc
            m_s[s, h] = jnp.broadcast_to(top, (rows, dim))
            l_s[s, h] = jnp.broadcast_to(norm, (rows, dim))
            out_ref[s, :, h * width : (h + 1) * width] = to_lanes(acc / norm, steps)
        return carry

    lax.fori_loop(0, slots, one_slot, 0)

    for copy in note_sends:
        copy.wait()
    total = note[per]
    for k in range(n - 1):
        total = total + notes[k, per]
    load_ref[...] = note[per] * n / total
    row_of = lax.broadcasted_iota(jnp.int32, (8, 128), 0)
    for j in range(per):
        slot = arrival_slots[j]
        length = lengths[slot]
        start = lax.div(length - 1, block_len) * block_len
        q_out[j] = qs[slot]
        acc_out[j] = acc_s[slot]
        m_out[j] = m_s[slot]
        l_out[j] = l_s[slot]
        info = jnp.where(lane[:8] + start < length, 0.0, NEG)
        info = jnp.where(row_of == 1, slot.astype(jnp.float32), info)
        for kv in range(2):
            for h in range(heads):
                info = jnp.where(
                    row_of == 2 + kv * heads + h, notes[j, j][kv : kv + 1, h : h + 1], info
                )
        info_ref[j] = info
    for copy in sends:
        copy.wait()


def merge_kernel(
    n, att, arrived, q, acc_in, m_in, l_in, info, load_tile,
    out_ref, landed_hbm, arrival_ref, load_ref, land_sem,
):
    me = lax.axis_index("inst")
    slots, steps, _ = att.shape
    per, heads, rows, dim = q.shape
    width = rows // steps * dim
    scaling = 1.0 / math.sqrt(dim)
    arrival_rows = [lax.rem(me + n - 1 - j, n) * per + j for j in range(per)]
    total_rows = n * per
    ranks = []
    for j in range(per):
        rank = 0
        for i in range(per):
            if i != j:
                rank = rank + (arrival_rows[j] - arrival_rows[i] + total_rows) // total_rows
        ranks.append(rank)
    copies = [
        pltpu.make_async_copy(arrived.at[j], landed_hbm.at[ranks[j]], land_sem.at[j])
        for j in range(per)
    ]
    for copy in copies:
        copy.start()
    load_ref[0] = load_tile[...][0, 0]
    lane = lax.broadcasted_iota(jnp.int32, (2, heads), 1)
    kv_of = lax.broadcasted_iota(jnp.int32, (2, heads), 0)
    for j in range(per):
        tile = jnp.zeros((2, heads), jnp.float32)
        for kv in range(2):
            for h in range(heads):
                r = 2 + kv * heads + h
                tile = jnp.where((kv_of == kv) & (lane == h), info[j, r : r + 1, 0:1], tile)
        arrival_ref[ranks[j]] = tile.astype(jnp.bfloat16)
    for h in range(heads):
        merged = []
        for j in range(per):
            raw = lax.dot_general(
                q[j, h], arrived[j, 0, h], TRANS, preferred_element_type=jnp.float32
            )
            x = raw * (info[j, 2 + h : 3 + h, :] * scaling)
            x = jnp.where(info[j, 0:1, :] < 0.0, NEG, x)
            old = m_in[j, h]
            top = jnp.maximum(old, jnp.max(x, axis=1, keepdims=True))
            fade = jnp.exp(old - top)
            p = jnp.exp(x - top)
            norm = l_in[j, h] * fade + jnp.sum(p, axis=1, keepdims=True)
            r = 2 + heads + h
            acc = acc_in[j, h] * fade + jnp.dot(
                (p * info[j, r : r + 1, :]).astype(jnp.bfloat16), arrived[j, 1, h],
                preferred_element_type=jnp.float32,
            )
            merged.append(to_lanes(acc / norm, steps))
        for s in range(slots):
            part = (s, slice(None), slice(h * width, (h + 1) * width))
            value = att[part]
            for j in range(per):
                hit = jnp.broadcast_to(info[j, 1:2, 0:1], merged[j].shape) == float(s)
                value = jnp.where(hit, merged[j], value)
            out_ref[part] = value
    for copy in copies:
        copy.wait()


def local(pool, scale, lengths, table, moves, queries, new_kv):
    n = lax.axis_size("inst")
    per = moves.shape[0] // n
    slots, steps, _ = queries.shape
    heads, block_len, dim = pool.shape[2:]
    rows = queries.shape[2] // (heads * dim) * steps
    hbm = functools.partial(pltpu.with_memory_space_constraint, memory_space=pltpu.HBM)
    any_space = pl.BlockSpec(memory_space=pl.ANY)
    smem = pl.BlockSpec(memory_space=pltpu.SMEM)
    vmem = pl.BlockSpec(memory_space=pltpu.VMEM)
    bf16, f32 = jnp.bfloat16, jnp.float32
    outs = (
        jax.ShapeDtypeStruct(queries.shape, bf16),
        jax.ShapeDtypeStruct((per,) + pool.shape[1:], bf16),
        jax.ShapeDtypeStruct((per, 2, heads), bf16),
        jax.ShapeDtypeStruct((1,), f32),
    )
    state = jax.ShapeDtypeStruct((per, heads, rows, dim), f32)
    results = pl.pallas_call(
        functools.partial(kernel, n),
        out_shape=(
            jax.ShapeDtypeStruct(queries.shape, bf16),
            jax.ShapeDtypeStruct((per,) + pool.shape[1:], bf16),
            jax.ShapeDtypeStruct((per, heads, rows, dim), bf16),
            state, state, state,
            jax.ShapeDtypeStruct((per, 8, 128), f32),
            jax.ShapeDtypeStruct((8, 128), f32),
        ),
        in_specs=[any_space] * 7,
        out_specs=(vmem,) * 8,
        scratch_shapes=[
            pltpu.VMEM(pool.shape, bf16),
            pltpu.VMEM(scale.shape[1:] + scale.shape[:1], bf16),
            pltpu.SMEM(lengths.shape, jnp.int32),
            pltpu.SMEM(table.shape[::-1], jnp.int32),
            pltpu.SMEM(moves.shape[::-1], jnp.int32),
            pltpu.VMEM(queries.shape, bf16),
            pltpu.VMEM(new_kv.shape, bf16),
            pltpu.VMEM((per,) + pool.shape[1:], bf16),
            pltpu.VMEM((per + 1, 8, 128), f32),
            pltpu.VMEM((n - 1, per + 1, 8, 128), f32),
            pltpu.VMEM((slots, heads, rows, dim), bf16),
            pltpu.VMEM((slots, heads, rows, dim), f32),
            pltpu.VMEM((slots, heads, rows, dim), f32),
            pltpu.VMEM((slots, heads, rows, dim), f32),
            pltpu.SemaphoreType.DMA,
            pltpu.SemaphoreType.DMA((6,)),
            pltpu.SemaphoreType.DMA((per, 2)),
            pltpu.SemaphoreType.DMA((per, 2)),
            pltpu.SemaphoreType.DMA((n - 1,)),
            pltpu.SemaphoreType.DMA((n - 1,)),
        ],
        compiler_params=pltpu.CompilerParams(
            collective_id=0, has_side_effects=True, vmem_limit_bytes=32 * 1024 * 1024
        ),
    )(
        hbm(pool), hbm(jnp.transpose(scale, (1, 2, 0))), hbm(lengths), hbm(table.T), hbm(moves.T),
        hbm(queries), hbm(new_kv),
    )
    return pl.pallas_call(
        functools.partial(merge_kernel, n),
        out_shape=outs,
        in_specs=[vmem] * 8,
        out_specs=(vmem, any_space, vmem, smem),
        scratch_shapes=[pltpu.SemaphoreType.DMA((per,))],
        compiler_params=pltpu.CompilerParams(vmem_limit_bytes=32 * 1024 * 1024),
    )(*results)


def solution(mesh):
    both = ("groups", "inst")
    return jax.shard_map(
        local,
        mesh=mesh,
        in_specs=(
            P(both, None, "tp", None, None),
            P(both, None, "tp"),
            P(both),
            P(both, None),
            P("groups", None),
            P(both, None, "tp"),
            P(both, None, None, "tp"),
        ),
        out_specs=(
            P(both, None, "tp"),
            P(both, None, "tp", None, None),
            P(both, None, "tp"),
            P(both),
        ),
        check_vma=False,
    )
```

```python
import functools
import math

import jax
import jax.numpy as jnp
from jax import lax
from jax.experimental import pallas as pl
from jax.experimental.pallas import tpu as pltpu
from jax.sharding import PartitionSpec as P

NEG = -1e30
TRANS = (((1,), (1,)), ((), ()))


def to_lanes(o, steps):
    return jnp.concatenate(
        [o[i : i + steps] for i in range(0, o.shape[0], steps)], axis=1
    ).astype(jnp.bfloat16)


def kernel(
    n, pool_hbm, scale_hbm, lengths_hbm, table_hbm, moves_hbm, q_hbm, new_hbm,
    out_ref, arrived, p_out, acc_out, info_ref, arrival_ref, load_ref,
    pool, scale, lengths, table, moves, q_ref, new_ref, staged, note, notes, qs, acc_s, m_s, l_s,
    pool_sem, in_sem, send_sem, recv_sem, note_send, note_recv,
):
    me = lax.axis_index("inst")
    slots, steps, _ = q_ref.shape
    per = staged.shape[0]
    blocks = table.shape[0]
    heads, block_len, dim = pool.shape[2:]
    group = q_ref.shape[2] // (heads * dim)
    rows = group * steps
    width = group * dim
    scaling = 1.0 / math.sqrt(dim)

    pieces = pool_sem.shape[0]
    edges = [pool.shape[0] * i // pieces for i in range(pieces + 1)]
    pool_copies = []
    for i in range(pieces):
        part = pl.ds(edges[i], edges[i + 1] - edges[i])
        pool_copies.append(
            pltpu.make_async_copy(pool_hbm.at[part], pool.at[part], pool_sem.at[i])
        )
    for copy in pool_copies:
        copy.start()
    barrier = pltpu.get_barrier_semaphore()
    for k in range(1, n):
        pl.semaphore_signal(
            barrier, inc=1, device_id={"inst": lax.rem(me + k, n)},
            device_id_type=pl.DeviceIdType.MESH,
        )
    small = [
        pltpu.make_async_copy(x, y, in_sem.at[3 + i])
        for i, (x, y) in enumerate(
            ((moves_hbm, moves), (lengths_hbm, lengths), (table_hbm, table))
        )
    ]
    for copy in small:
        copy.start()
    scale_copy = pltpu.make_async_copy(scale_hbm, scale, in_sem.at[0])
    scale_copy.start()
    q_copy = pltpu.make_async_copy(q_hbm, q_ref, in_sem.at[1])
    q_copy.start()
    new_copy = pltpu.make_async_copy(new_hbm, new_ref, in_sem.at[2])
    new_copy.start()

    for copy in small:
        copy.wait()

    tokens = jnp.float32(0.0)
    for s in range(slots):
        tokens = tokens + (lengths[s] + steps).astype(jnp.float32)
    note[per] = jnp.full((8, 128), tokens, jnp.float32)
    scale_copy.wait()
    scale_rows = jnp.concatenate(
        [scale[kv].astype(jnp.float32) for kv in range(2)], axis=0
    )
    block_of = lax.broadcasted_iota(jnp.int32, scale_rows.shape, 1)

    def block_scale(index):
        return jnp.sum(
            jnp.where(block_of == index, scale_rows, 0.0), axis=1, keepdims=True
        )

    head_lane = lax.broadcasted_iota(jnp.int32, (1, 128), 1)
    for j in range(per):
        pair = block_scale(moves[0, me * per + j])
        for kv in range(2):
            row = jnp.zeros((1, 128), jnp.float32)
            for h in range(heads):
                r = kv * heads + h
                row = jnp.where(head_lane == h, pair[r : r + 1], row)
            note[j, pl.ds(kv, 1), :] = row
    for copy in pool_copies:
        copy.wait()
    for j in range(per):
        staged[j] = pool[moves[0, me * per + j]]
    pl.semaphore_wait(barrier, n - 1)

    sends = []
    for j in range(per):
        for kv in range(2):
            sends.append(
                pltpu.make_async_remote_copy(
                    src_ref=staged.at[j, kv], dst_ref=arrived.at[j, kv],
                    send_sem=send_sem.at[j, kv], recv_sem=recv_sem.at[j, kv],
                    device_id={"inst": lax.rem(me + 1 + j, n)},
                    device_id_type=pl.DeviceIdType.MESH,
                )
            )
    note_sends = []
    for k in range(1, n):
        note_sends.append(
            pltpu.make_async_remote_copy(
                src_ref=note, dst_ref=notes.at[k - 1],
                send_sem=note_send.at[k - 1], recv_sem=note_recv.at[k - 1],
                device_id={"inst": lax.rem(me + k, n)},
                device_id_type=pl.DeviceIdType.MESH,
            )
        )
    for copy in note_sends + sends[:2]:
        copy.start()
    last = me == n - 1

    @pl.when(jnp.logical_not(last))
    def _():
        for copy in sends[2:]:
            copy.start()

    sources = [lax.rem(me + n - 1 - j, n) for j in range(per)]
    arrival_rows = [sources[j] * per + j for j in range(per)]
    arrival_slots = [moves[2, arrival_rows[j]] for j in range(per)]

    lane = lax.broadcasted_iota(jnp.int32, (rows, block_len), 1)
    step_of = lax.broadcasted_iota(jnp.int32, (rows, block_len), 0) % steps
    causal = lane <= step_of
    q_copy.wait()
    new_copy.wait()

    def one_slot(s, carry):
        length = lengths[s]
        count = lax.div(length + (block_len - 1), block_len)
        hit = arrival_slots[0] == s
        for j in range(1, per):
            hit = jnp.logical_or(hit, arrival_slots[j] == s)
        limit = jnp.where(hit, (count - 1) * block_len, length)
        q_all = q_ref[s].astype(jnp.float32)
        fresh = [new_ref[s, u].astype(jnp.float32) for u in range(steps)]
        index = [jnp.clip(table[j, s], 0, pool.shape[0] - 1) for j in range(blocks)]
        scales = [block_scale(index[j]) for j in range(blocks)]
        pad = jnp.zeros((block_len - steps, dim), jnp.float32)
        for h in range(heads):
            lo = h * group * dim
            qh = jnp.concatenate(
                [q_all[:, lo + g * dim : lo + (g + 1) * dim] for g in range(group)], axis=0
            ).astype(jnp.bfloat16)
            qs[s, h] = qh
            new_k, new_v = [
                jnp.concatenate(
                    [f[kv : kv + 1, h * dim : (h + 1) * dim] for f in fresh] + [pad], axis=0
                ).astype(jnp.bfloat16)
                for kv in range(2)
            ]
            scored = []
            for j in range(blocks):
                raw = lax.dot_general(
                    qh, pool[index[j], 0, h], TRANS, preferred_element_type=jnp.float32
                )
                raw = raw * (scales[j][h : h + 1] * scaling)
                scored.append(jnp.where(lane + j * block_len < limit, raw, NEG))
            raw = lax.dot_general(qh, new_k, TRANS, preferred_element_type=jnp.float32)
            scored.append(jnp.where(causal, raw * scaling, NEG))
            top = scored[0]
            for x in scored[1:]:
                top = jnp.maximum(top, x)
            top = jnp.max(top, axis=1, keepdims=True)
            p = [jnp.exp(x - top) for x in scored]
            norm = p[0]
            for x in p[1:]:
                norm = norm + x
            norm = jnp.sum(norm, axis=1, keepdims=True)
            acc = jnp.dot(p[-1].astype(jnp.bfloat16), new_v, preferred_element_type=jnp.float32)
            for j in range(blocks):
                w = (p[j] * scales[j][heads + h : heads + h + 1]).astype(jnp.bfloat16)
                acc = acc + jnp.dot(
                    w, pool[index[j], 1, h], preferred_element_type=jnp.float32
                )
            acc_s[s, h] = acc
            m_s[s, h] = jnp.broadcast_to(top, (rows, dim))
            l_s[s, h] = jnp.broadcast_to(norm, (rows, dim))
            out_ref[s, :, h * width : (h + 1) * width] = to_lanes(acc / norm, steps)
        return carry

    held = slots * 7 // 8
    lax.fori_loop(0, held, one_slot, 0)

    @pl.when(last)
    def _():
        for copy in sends[2:]:
            copy.start()

    if held < slots:
        lax.fori_loop(held, slots, one_slot, 0)

    for copy in note_sends:
        copy.wait()
    total = note[per]
    for k in range(n - 1):
        total = total + notes[k, per]
    load_ref[...] = note[per] * n / total
    total_rows = n * per
    ranks = []
    for j in range(per):
        rank = 0
        for i in range(per):
            if i != j:
                rank = rank + (arrival_rows[j] - arrival_rows[i] + total_rows) // total_rows
        ranks.append(rank)
    for j in range(per):
        slot = arrival_slots[j]
        length = lengths[slot]
        start = lax.div(length - 1, block_len) * block_len
        info_ref[j] = jnp.full((8, 128), slot.astype(jnp.float32), jnp.float32)
        tile = notes[j, j]
        arrival_ref[ranks[j]] = tile[:2, :heads].astype(jnp.bfloat16)
        sends[2 * j].wait_recv()
        for h in range(heads):
            raw = lax.dot_general(
                qs[slot, h], arrived[j, 0, h], TRANS, preferred_element_type=jnp.float32
            )
            x = jnp.where(lane + start < length, raw * (tile[0:1, h : h + 1] * scaling), NEG)
            old = m_s[slot, h]
            top = jnp.maximum(old, jnp.max(x, axis=1, keepdims=True))
            fade = jnp.exp(old - top)
            p = jnp.exp(x - top)
            norm = l_s[slot, h] * fade + jnp.sum(p, axis=1, keepdims=True)
            p_out[j, h] = (p * (tile[1:2, h : h + 1] / norm)).astype(jnp.bfloat16)
            acc_out[j, h] = acc_s[slot, h] * (fade / norm)
    for j in range(per):
        sends[2 * j + 1].wait_recv()
    for copy in sends:
        copy.wait_send()


def merge_kernel(
    n, att, arrived, p_in, acc_in, info, arrival, load_tile,
    out_hbm, landed_hbm, arrival_hbm, load_hbm, out_ref, load_ref, land_sem, small_sem, out_sem,
):
    me = lax.axis_index("inst")
    slots, steps, _ = att.shape
    per, heads, rows, dim = p_in.shape
    width = rows // steps * dim
    arrival_rows = [lax.rem(me + n - 1 - j, n) * per + j for j in range(per)]
    total_rows = n * per
    ranks = []
    for j in range(per):
        rank = 0
        for i in range(per):
            if i != j:
                rank = rank + (arrival_rows[j] - arrival_rows[i] + total_rows) // total_rows
        ranks.append(rank)
    copies = [
        pltpu.make_async_copy(arrived.at[j], landed_hbm.at[ranks[j]], land_sem.at[j])
        for j in range(per)
    ]
    copies.append(pltpu.make_async_copy(arrival, arrival_hbm, small_sem.at[0]))
    for copy in copies:
        copy.start()
    load_ref[0] = load_tile[...][0, 0]
    load_copy = pltpu.make_async_copy(load_ref, load_hbm, small_sem.at[1])
    load_copy.start()
    copies.append(load_copy)
    for h in range(heads):
        merged = [
            to_lanes(
                acc_in[j, h]
                + jnp.dot(p_in[j, h], arrived[j, 1, h], preferred_element_type=jnp.float32),
                steps,
            )
            for j in range(per)
        ]
        for s in range(slots):
            part = (s, slice(None), slice(h * width, (h + 1) * width))
            value = att[part]
            for j in range(per):
                hit = jnp.broadcast_to(info[j, 1:2, 0:1], merged[j].shape) == float(s)
                value = jnp.where(hit, merged[j], value)
            out_ref[part] = value
        half = (slice(None), slice(None), pl.ds(h * width, width))
        copy = pltpu.make_async_copy(out_ref.at[half], out_hbm.at[half], out_sem.at[h])
        copy.start()
        copies.append(copy)
    for copy in copies:
        copy.wait()


def local(pool, scale, lengths, table, moves, queries, new_kv):
    n = lax.axis_size("inst")
    per = moves.shape[0] // n
    slots, steps, _ = queries.shape
    heads, block_len, dim = pool.shape[2:]
    rows = queries.shape[2] // (heads * dim) * steps
    hbm = functools.partial(pltpu.with_memory_space_constraint, memory_space=pltpu.HBM)
    any_space = pl.BlockSpec(memory_space=pl.ANY)
    vmem = pl.BlockSpec(memory_space=pltpu.VMEM)
    bf16, f32 = jnp.bfloat16, jnp.float32
    outs = (
        jax.ShapeDtypeStruct(queries.shape, bf16),
        jax.ShapeDtypeStruct((per,) + pool.shape[1:], bf16),
        jax.ShapeDtypeStruct((per, 2, heads), bf16),
        jax.ShapeDtypeStruct((1,), f32),
    )
    results = pl.pallas_call(
        functools.partial(kernel, n),
        out_shape=(
            jax.ShapeDtypeStruct(queries.shape, bf16),
            jax.ShapeDtypeStruct((per,) + pool.shape[1:], bf16),
            jax.ShapeDtypeStruct((per, heads, rows, dim), bf16),
            jax.ShapeDtypeStruct((per, heads, rows, dim), f32),
            jax.ShapeDtypeStruct((per, 8, 128), f32),
            outs[2],
            jax.ShapeDtypeStruct((8, 128), f32),
        ),
        in_specs=[any_space] * 7,
        out_specs=(vmem,) * 7,
        scratch_shapes=[
            pltpu.VMEM(pool.shape, bf16),
            pltpu.VMEM(scale.shape[1:] + scale.shape[:1], bf16),
            pltpu.SMEM(lengths.shape, jnp.int32),
            pltpu.SMEM(table.shape[::-1], jnp.int32),
            pltpu.SMEM(moves.shape[::-1], jnp.int32),
            pltpu.VMEM(queries.shape, bf16),
            pltpu.VMEM(new_kv.shape, bf16),
            pltpu.VMEM((per,) + pool.shape[1:], bf16),
            pltpu.VMEM((per + 1, 8, 128), f32),
            pltpu.VMEM((n - 1, per + 1, 8, 128), f32),
            pltpu.VMEM((slots, heads, rows, dim), bf16),
            pltpu.VMEM((slots, heads, rows, dim), f32),
            pltpu.VMEM((slots, heads, rows, dim), f32),
            pltpu.VMEM((slots, heads, rows, dim), f32),
            pltpu.SemaphoreType.DMA((1,)),
            pltpu.SemaphoreType.DMA((6,)),
            pltpu.SemaphoreType.DMA((per, 2)),
            pltpu.SemaphoreType.DMA((per, 2)),
            pltpu.SemaphoreType.DMA((n - 1,)),
            pltpu.SemaphoreType.DMA((n - 1,)),
        ],
        compiler_params=pltpu.CompilerParams(
            collective_id=0, has_side_effects=True, vmem_limit_bytes=32 * 1024 * 1024
        ),
    )(
        hbm(pool), hbm(jnp.transpose(scale, (1, 2, 0))), hbm(lengths), hbm(table.T), hbm(moves.T),
        hbm(queries), hbm(new_kv),
    )
    return pl.pallas_call(
        functools.partial(merge_kernel, n),
        out_shape=outs,
        in_specs=[vmem] * 7,
        out_specs=(any_space,) * 4,
        scratch_shapes=[
            pltpu.VMEM(queries.shape, bf16),
            pltpu.SMEM((1,), f32),
            pltpu.SemaphoreType.DMA((per,)),
            pltpu.SemaphoreType.DMA((2,)),
            pltpu.SemaphoreType.DMA((heads,)),
        ],
        compiler_params=pltpu.CompilerParams(vmem_limit_bytes=32 * 1024 * 1024),
    )(*results)


def solution(mesh):
    both = ("groups", "inst")
    return jax.shard_map(
        local,
        mesh=mesh,
        in_specs=(
            P(both, None, "tp", None, None),
            P(both, None, "tp"),
            P(both),
            P(both, None),
            P("groups", None),
            P(both, None, "tp"),
            P(both, None, None, "tp"),
        ),
        out_specs=(
            P(both, None, "tp"),
            P(both, None, "tp", None, None),
            P(both, None, "tp"),
            P(both),
        ),
        check_vma=False,
    )
```

```python
import functools
import math

import jax
import jax.numpy as jnp
from jax import lax
from jax.experimental import pallas as pl
from jax.experimental.pallas import tpu as pltpu
from jax.sharding import PartitionSpec as P

NEG = -1e30
TRANS = (((1,), (1,)), ((), ()))


def to_lanes(o, steps):
    return jnp.concatenate(
        [o[i : i + steps] for i in range(0, o.shape[0], steps)], axis=1
    ).astype(jnp.bfloat16)


def kernel(
    n, pool_hbm, scale_hbm, lengths_hbm, table_hbm, moves_hbm, q_hbm, new_hbm,
    out_ref, arrived, p_out, acc_out, info_ref, arrival_ref, load_ref,
    keys, values, scale, lengths, table, moves, q_ref, new_ref, staged, note, notes, qs, acc_s, m_s, l_s,
    pool_sem, in_sem, send_sem, recv_sem, note_send, note_recv,
):
    me = lax.axis_index("inst")
    slots, steps, _ = q_ref.shape
    per = staged.shape[0]
    blocks = table.shape[0]
    heads, block_len, dim = keys.shape[1:]
    group = q_ref.shape[2] // (heads * dim)
    rows = group * steps
    width = group * dim
    scaling = 1.0 / math.sqrt(dim)

    small = [
        pltpu.make_async_copy(x, y, in_sem.at[3 + i])
        for i, (x, y) in enumerate(
            ((moves_hbm, moves), (lengths_hbm, lengths), (table_hbm, table))
        )
    ]
    for copy in small:
        copy.start()
    scale_copy = pltpu.make_async_copy(scale_hbm, scale, in_sem.at[0])
    scale_copy.start()
    pool_copies = [
        pltpu.make_async_copy(pool_hbm.at[:, kv], part, pool_sem.at[kv])
        for kv, part in enumerate((keys, values))
    ]
    pool_copies[0].start()
    pool_copies[1].start()
    q_copy = pltpu.make_async_copy(q_hbm, q_ref, in_sem.at[1])
    q_copy.start()
    new_copy = pltpu.make_async_copy(new_hbm, new_ref, in_sem.at[2])
    new_copy.start()

    barrier = pltpu.get_barrier_semaphore()
    for k in range(1, n):
        pl.semaphore_signal(
            barrier, inc=1, device_id={"inst": lax.rem(me + k, n)},
            device_id_type=pl.DeviceIdType.MESH,
        )
    for copy in small:
        copy.wait()

    tokens = jnp.float32(0.0)
    for s in range(slots):
        tokens = tokens + (lengths[s] + steps).astype(jnp.float32)
    note[per] = jnp.full((8, 128), tokens, jnp.float32)
    scale_copy.wait()
    scale_rows = jnp.concatenate(
        [scale[kv].astype(jnp.float32) for kv in range(2)], axis=0
    )
    block_of = lax.broadcasted_iota(jnp.int32, scale_rows.shape, 1)

    def block_scale(index):
        return jnp.sum(
            jnp.where(block_of == index, scale_rows, 0.0), axis=1, keepdims=True
        )

    head_lane = lax.broadcasted_iota(jnp.int32, (1, 128), 1)
    for j in range(per):
        pair = block_scale(moves[0, me * per + j])
        for kv in range(2):
            row = jnp.zeros((1, 128), jnp.float32)
            for h in range(heads):
                r = kv * heads + h
                row = jnp.where(head_lane == h, pair[r : r + 1], row)
            note[j, pl.ds(kv, 1), :] = row
    pool_copies[0].wait()
    for j in range(per):
        staged[j, 0] = keys[moves[0, me * per + j]]
    pl.semaphore_wait(barrier, n - 1)

    sends = []
    for j in range(per):
        for kv in range(2):
            sends.append(
                pltpu.make_async_remote_copy(
                    src_ref=staged.at[j, kv], dst_ref=arrived.at[j, kv],
                    send_sem=send_sem.at[j, kv], recv_sem=recv_sem.at[j, kv],
                    device_id={"inst": lax.rem(me + 1 + j, n)},
                    device_id_type=pl.DeviceIdType.MESH,
                )
            )
    note_sends = []
    for k in range(1, n):
        note_sends.append(
            pltpu.make_async_remote_copy(
                src_ref=note, dst_ref=notes.at[k - 1],
                send_sem=note_send.at[k - 1], recv_sem=note_recv.at[k - 1],
                device_id={"inst": lax.rem(me + k, n)},
                device_id_type=pl.DeviceIdType.MESH,
            )
        )
    last = me == n - 1

    def begin(kv):
        sends[kv].start()

        @pl.when(jnp.logical_not(last))
        def _():
            for j in range(1, per):
                sends[2 * j + kv].start()

    for copy in note_sends:
        copy.start()
    begin(0)
    pool_copies[1].wait()
    for j in range(per):
        staged[j, 1] = values[moves[0, me * per + j]]
    begin(1)

    sources = [lax.rem(me + n - 1 - j, n) for j in range(per)]
    arrival_rows = [sources[j] * per + j for j in range(per)]
    arrival_slots = [moves[2, arrival_rows[j]] for j in range(per)]

    lane = lax.broadcasted_iota(jnp.int32, (rows, block_len), 1)
    step_of = lax.broadcasted_iota(jnp.int32, (rows, block_len), 0) % steps
    causal = lane <= step_of
    q_copy.wait()
    new_copy.wait()

    def one_slot(s, carry):
        length = lengths[s]
        count = lax.div(length + (block_len - 1), block_len)
        hit = arrival_slots[0] == s
        for j in range(1, per):
            hit = jnp.logical_or(hit, arrival_slots[j] == s)
        limit = jnp.where(hit, (count - 1) * block_len, length)
        q_all = q_ref[s].astype(jnp.float32)
        fresh = [new_ref[s, u].astype(jnp.float32) for u in range(steps)]
        index = [jnp.clip(table[j, s], 0, keys.shape[0] - 1) for j in range(blocks)]
        scales = [block_scale(index[j]) for j in range(blocks)]
        pad = jnp.zeros((block_len - steps, dim), jnp.float32)
        for h in range(heads):
            lo = h * group * dim
            qh = jnp.concatenate(
                [q_all[:, lo + g * dim : lo + (g + 1) * dim] for g in range(group)], axis=0
            ).astype(jnp.bfloat16)
            qs[s, h] = qh
            new_k, new_v = [
                jnp.concatenate(
                    [f[kv : kv + 1, h * dim : (h + 1) * dim] for f in fresh] + [pad], axis=0
                ).astype(jnp.bfloat16)
                for kv in range(2)
            ]
            scored = []
            for j in range(blocks):
                raw = lax.dot_general(
                    qh, keys[index[j], h], TRANS, preferred_element_type=jnp.float32
                )
                raw = raw * (scales[j][h : h + 1] * scaling)
                scored.append(jnp.where(lane + j * block_len < limit, raw, NEG))
            raw = lax.dot_general(qh, new_k, TRANS, preferred_element_type=jnp.float32)
            scored.append(jnp.where(causal, raw * scaling, NEG))
            top = scored[0]
            for x in scored[1:]:
                top = jnp.maximum(top, x)
            top = jnp.max(top, axis=1, keepdims=True)
            p = [jnp.exp(x - top) for x in scored]
            norm = p[0]
            for x in p[1:]:
                norm = norm + x
            norm = jnp.sum(norm, axis=1, keepdims=True)
            acc = jnp.dot(p[-1].astype(jnp.bfloat16), new_v, preferred_element_type=jnp.float32)
            for j in range(blocks):
                w = (p[j] * scales[j][heads + h : heads + h + 1]).astype(jnp.bfloat16)
                acc = acc + jnp.dot(
                    w, values[index[j], h], preferred_element_type=jnp.float32
                )
            acc_s[s, h] = acc
            m_s[s, h] = jnp.broadcast_to(top, (rows, dim))
            l_s[s, h] = jnp.broadcast_to(norm, (rows, dim))
            out_ref[s, :, h * width : (h + 1) * width] = to_lanes(acc / norm, steps)
        return carry

    held = slots * 7 // 8
    lax.fori_loop(0, held, one_slot, 0)

    @pl.when(last)
    def _():
        for copy in sends[2:]:
            copy.start()

    if held < slots:
        lax.fori_loop(held, slots, one_slot, 0)

    for copy in note_sends:
        copy.wait()
    total = note[per]
    for k in range(n - 1):
        total = total + notes[k, per]
    load_ref[...] = note[per] * n / total
    total_rows = n * per
    ranks = []
    for j in range(per):
        rank = 0
        for i in range(per):
            if i != j:
                rank = rank + (arrival_rows[j] - arrival_rows[i] + total_rows) // total_rows
        ranks.append(rank)
    for j in range(per):
        slot = arrival_slots[j]
        length = lengths[slot]
        start = lax.div(length - 1, block_len) * block_len
        info_ref[j] = jnp.full((8, 128), slot.astype(jnp.float32), jnp.float32)
        tile = notes[j, j]
        arrival_ref[ranks[j]] = tile[:2, :heads].astype(jnp.bfloat16)
        sends[2 * j].wait_recv()
        for h in range(heads):
            raw = lax.dot_general(
                qs[slot, h], arrived[j, 0, h], TRANS, preferred_element_type=jnp.float32
            )
            x = jnp.where(lane + start < length, raw * (tile[0:1, h : h + 1] * scaling), NEG)
            old = m_s[slot, h]
            top = jnp.maximum(old, jnp.max(x, axis=1, keepdims=True))
            fade = jnp.exp(old - top)
            p = jnp.exp(x - top)
            norm = l_s[slot, h] * fade + jnp.sum(p, axis=1, keepdims=True)
            p_out[j, h] = (p * (tile[1:2, h : h + 1] / norm)).astype(jnp.bfloat16)
            acc_out[j, h] = acc_s[slot, h] * (fade / norm)
    for j in range(per):
        sends[2 * j + 1].wait_recv()
    for copy in sends:
        copy.wait_send()


def merge_kernel(
    n, att, arrived, p_in, acc_in, info, arrival, load_tile,
    out_hbm, landed_hbm, arrival_hbm, load_hbm, out_ref, load_ref, land_sem, small_sem, out_sem,
):
    me = lax.axis_index("inst")
    slots, steps, _ = att.shape
    per, heads, rows, dim = p_in.shape
    width = rows // steps * dim
    arrival_rows = [lax.rem(me + n - 1 - j, n) * per + j for j in range(per)]
    total_rows = n * per
    ranks = []
    for j in range(per):
        rank = 0
        for i in range(per):
            if i != j:
                rank = rank + (arrival_rows[j] - arrival_rows[i] + total_rows) // total_rows
        ranks.append(rank)
    copies = [
        pltpu.make_async_copy(arrived.at[j], landed_hbm.at[ranks[j]], land_sem.at[j])
        for j in range(per)
    ]
    copies.append(pltpu.make_async_copy(arrival, arrival_hbm, small_sem.at[0]))
    for copy in copies:
        copy.start()
    load_ref[0] = load_tile[...][0, 0]
    load_copy = pltpu.make_async_copy(load_ref, load_hbm, small_sem.at[1])
    load_copy.start()
    copies.append(load_copy)
    for h in range(heads):
        merged = [
            to_lanes(
                acc_in[j, h]
                + jnp.dot(p_in[j, h], arrived[j, 1, h], preferred_element_type=jnp.float32),
                steps,
            )
            for j in range(per)
        ]
        for s in range(slots):
            part = (s, slice(None), slice(h * width, (h + 1) * width))
            value = att[part]
            for j in range(per):
                hit = jnp.broadcast_to(info[j, 1:2, 0:1], merged[j].shape) == float(s)
                value = jnp.where(hit, merged[j], value)
            out_ref[part] = value
        half = (slice(None), slice(None), pl.ds(h * width, width))
        copy = pltpu.make_async_copy(out_ref.at[half], out_hbm.at[half], out_sem.at[h])
        copy.start()
        copies.append(copy)
    for copy in copies:
        copy.wait()


def local(pool, scale, lengths, table, moves, queries, new_kv):
    n = lax.axis_size("inst")
    per = moves.shape[0] // n
    slots, steps, _ = queries.shape
    heads, block_len, dim = pool.shape[2:]
    rows = queries.shape[2] // (heads * dim) * steps
    hbm = functools.partial(pltpu.with_memory_space_constraint, memory_space=pltpu.HBM)
    any_space = pl.BlockSpec(memory_space=pl.ANY)
    vmem = pl.BlockSpec(memory_space=pltpu.VMEM)
    bf16, f32 = jnp.bfloat16, jnp.float32
    outs = (
        jax.ShapeDtypeStruct(queries.shape, bf16),
        jax.ShapeDtypeStruct((per,) + pool.shape[1:], bf16),
        jax.ShapeDtypeStruct((per, 2, heads), bf16),
        jax.ShapeDtypeStruct((1,), f32),
    )
    results = pl.pallas_call(
        functools.partial(kernel, n),
        out_shape=(
            jax.ShapeDtypeStruct(queries.shape, bf16),
            jax.ShapeDtypeStruct((per,) + pool.shape[1:], bf16),
            jax.ShapeDtypeStruct((per, heads, rows, dim), bf16),
            jax.ShapeDtypeStruct((per, heads, rows, dim), f32),
            jax.ShapeDtypeStruct((per, 8, 128), f32),
            outs[2],
            jax.ShapeDtypeStruct((8, 128), f32),
        ),
        in_specs=[any_space] * 7,
        out_specs=(vmem,) * 7,
        scratch_shapes=[
            pltpu.VMEM(pool.shape[:1] + pool.shape[2:], bf16),
            pltpu.VMEM(pool.shape[:1] + pool.shape[2:], bf16),
            pltpu.VMEM(scale.shape[1:] + scale.shape[:1], bf16),
            pltpu.SMEM(lengths.shape, jnp.int32),
            pltpu.SMEM(table.shape[::-1], jnp.int32),
            pltpu.SMEM(moves.shape[::-1], jnp.int32),
            pltpu.VMEM(queries.shape, bf16),
            pltpu.VMEM(new_kv.shape, bf16),
            pltpu.VMEM((per,) + pool.shape[1:], bf16),
            pltpu.VMEM((per + 1, 8, 128), f32),
            pltpu.VMEM((n - 1, per + 1, 8, 128), f32),
            pltpu.VMEM((slots, heads, rows, dim), bf16),
            pltpu.VMEM((slots, heads, rows, dim), f32),
            pltpu.VMEM((slots, heads, rows, dim), f32),
            pltpu.VMEM((slots, heads, rows, dim), f32),
            pltpu.SemaphoreType.DMA((2,)),
            pltpu.SemaphoreType.DMA((6,)),
            pltpu.SemaphoreType.DMA((per, 2)),
            pltpu.SemaphoreType.DMA((per, 2)),
            pltpu.SemaphoreType.DMA((n - 1,)),
            pltpu.SemaphoreType.DMA((n - 1,)),
        ],
        compiler_params=pltpu.CompilerParams(
            collective_id=0, has_side_effects=True, vmem_limit_bytes=32 * 1024 * 1024
        ),
    )(
        hbm(pool), hbm(jnp.transpose(scale, (1, 2, 0))), hbm(lengths), hbm(table.T), hbm(moves.T),
        hbm(queries), hbm(new_kv),
    )
    return pl.pallas_call(
        functools.partial(merge_kernel, n),
        out_shape=outs,
        in_specs=[vmem] * 7,
        out_specs=(any_space,) * 4,
        scratch_shapes=[
            pltpu.VMEM(queries.shape, bf16),
            pltpu.SMEM((1,), f32),
            pltpu.SemaphoreType.DMA((per,)),
            pltpu.SemaphoreType.DMA((2,)),
            pltpu.SemaphoreType.DMA((heads,)),
        ],
        compiler_params=pltpu.CompilerParams(vmem_limit_bytes=32 * 1024 * 1024),
    )(*results)


def solution(mesh):
    both = ("groups", "inst")
    return jax.shard_map(
        local,
        mesh=mesh,
        in_specs=(
            P(both, None, "tp", None, None),
            P(both, None, "tp"),
            P(both),
            P(both, None),
            P("groups", None),
            P(both, None, "tp"),
            P(both, None, None, "tp"),
        ),
        out_specs=(
            P(both, None, "tp"),
            P(both, None, "tp", None, None),
            P(both, None, "tp"),
            P(both),
        ),
        check_vma=False,
    )
```
